768 devices in a mesh: row: 48 (over x, z), split: 16 (over y, core).
Axes of the slice: x: 4, y: 8, z: 12, core: 2. Of those that a mesh axis runs over, the one named last changes fastest.
Arguments:
- tiles: bfloat16 [73728, 4096], P(('row', 'split')), may hold values from -6 to 6
- tile_dest: int32 [73728, 1], P(('row', 'split')), may hold values from 0 to 47; in each aligned block of 96 rows (0 to 95, 96 to 191, ...) at most 3 rows name the same one
- tile_row: int32 [73728], P(('row', 'split')), may hold values from 0 to 31
- tile_col: int32 [73728], P(('row', 'split')), may hold values from 0 to 15
- density: bfloat16 [16384, 256], P('split'), may hold values from -0.109375 to 0.109375
Outputs:
- contracted: bfloat16 [98304, 256], P(('row', 'split'))
The draws below stay inside these ranges and needn't reach their ends.
Inputs may be any that keep to these rules, and one draw needn't show every extreme that they name: `tile_dest`: within the blocks of one device (aligned runs of 96 blocks) no row owner is named more than 3 times.
All inputs are finite; a program needn't handle non-finite values.
Results may differ from the reference program's by a relative error of at most 0.001.
Values may be sent and summed in bfloat16 or wider, within the bound.
A program may use at most 32 MiB of HBM per device.

```python
import math
import jax
import jax.numpy as jnp
import numpy as np
from jax import lax

B = 64
OCC = 256
TILES_DEV = 96
RBLK = 32
NUBLK = 16
CAP = 3
TILES = 73728
NU = 16384
N_ROW = 48
N_SPLIT = 16


def with_ends(result, key, low, high):
    extent = result.shape
    index_at = [jax.random.randint(jax.random.fold_in(key, axis), (), 0, extent[axis]) for axis in range(len(extent))]
    result = result.at[tuple(index_at)].set(low)
    longest = extent.index(max(extent))
    index_at[longest] = (index_at[longest] + 1) % extent[longest]
    return result.at[tuple(index_at)].set(high)


def level_of(key, extent, cuts, smallest, top_value):
    gain = 1.0
    for dim, blocks in cuts:
        draws = jax.random.uniform(jax.random.fold_in(jax.random.fold_in(key, 6), dim), (blocks,), jnp.float32, smallest / len(cuts), top_value / len(cuts))
        gain = gain * jnp.repeat(jnp.exp(draws), extent[dim] // blocks).reshape((-1,) + (1,) * (len(extent) - 1 - dim))
    return gain


def assign_block(key, own, number, rows, amount, top, limit, lean):
    sequence = jax.random.permutation(key, amount)
    crowded, usual = portions_of(amount, rows * top, limit, lean, True), portions_of(amount, rows * top, limit, lean, False)
    places = jnp.arange(amount)

    def named(sizes, turn):
        used = int((sizes > 0).sum())
        fixed = max(1, used // 4)
        passed = fixed + (places - fixed + turn * (used - fixed)) % max(1, amount - fixed)
        return jnp.zeros((amount,), jnp.int32).at[sequence[jnp.where(places < fixed, places, passed)]].set(jnp.asarray(sizes, jnp.int32))

    sizes = jnp.where(number % 4 == 0, named(crowded, number // 4), named(usual, number - number // 4 - 1))
    mixed = jax.random.permutation(jax.random.fold_in(own, 3), amount)
    source_of, receiver = mixed[0:amount // 2 * 2:2], mixed[1:amount // 2 * 2:2]
    slack = jnp.minimum(sizes[source_of] - 1, limit - sizes[receiver]) // 2
    slack = jnp.where((source_of == sequence[0]) | (receiver == sequence[0]) | (sizes[receiver] == 0), 0, jnp.maximum(slack, 0))
    passed = jax.random.randint(jax.random.fold_in(own, 4), (amount // 2,), 0, 1 << 20) % (slack + 1)
    sizes = sizes.at[source_of].add(-passed).at[receiver].add(passed)
    items = jnp.searchsorted(jnp.cumsum(sizes), jnp.arange(rows * top), side="right").astype(jnp.int32)
    listing = items.reshape(top, rows).T
    listing = listing[jax.random.permutation(jax.random.fold_in(own, 1), rows)]
    turn = jax.random.randint(jax.random.fold_in(own, 2), (rows, 1), 0, top)
    return jnp.take_along_axis(listing, (jnp.arange(top)[None, :] + turn) % top, axis=1)


def portions_of(amount, total, most, lean, full):
    loads = [(1 << 20) // math.isqrt(standing ** lean) + 1 for standing in range(1, amount + 1)]
    largest = most if full else min(most, max(-(-total // amount), total * loads[0] // sum(loads)))
    least = 1 if total - largest >= amount - 1 else 0
    given, surplus = [largest] + [least] * (amount - 1), total - largest - least * (amount - 1)
    while surplus > 0:
        free = [i for i in range(1, amount) if given[i] < largest] or [i for i in range(1, amount) if given[i] < most]
        mass, budget = sum([loads[i] for i in free]), surplus
        for i in free:
            addition = min(most - given[i], max(1, budget * loads[i] // mass), surplus)
            given[i] = given[i] + addition
            surplus = surplus - addition
    return np.array(given)


def centred(key, dims, spread, limit, shards=(), held_as=jnp.bfloat16):
    factor_of = level_of(key, dims, shards, -0.22, 0.18) if shards else 1.0
    result = jax.random.normal(key, dims, jnp.float32) * spread * factor_of
    return jnp.minimum(jnp.maximum(result, -limit), limit).astype(held_as)


def setup_inputs(seed: int = 0) -> dict:
    splits = jax.random.split(jax.random.key(seed), 6)
    tiles = centred(splits[0], (TILES, B * B), 1.0, 6.0, ((0, 768),))
    tile_dest_keys = jax.random.split(jax.random.fold_in(splits[1], 1), TILES // TILES_DEV)
    tile_dest_turns = jax.random.permutation(jax.random.fold_in(splits[1], 3), TILES // TILES_DEV)
    tile_dest = jax.vmap(lambda own, number: assign_block(jax.random.fold_in(splits[1], 2), own, number, TILES_DEV, N_ROW, 1, CAP, 2))(tile_dest_keys, tile_dest_turns).reshape((TILES, 1))
    tile_row = with_ends(jax.random.randint(splits[2], (TILES,), 0, RBLK), jax.random.fold_in(splits[2], 1), 0, RBLK - 1).astype(jnp.int32)
    tile_col = with_ends(jax.random.randint(splits[3], (TILES,), 0, NUBLK), jax.random.fold_in(splits[3], 1), 0, NUBLK - 1).astype(jnp.int32)
    density = centred(splits[4], (NU, OCC), (B * TILES_DEV * N_SPLIT // RBLK) ** -0.5, 0.109375, ((0, 16),))
    return dict(tiles=tiles, tile_dest=tile_dest, tile_row=tile_row, tile_col=tile_col, density=density)


def reference(tiles, tile_dest, tile_row, tile_col, density):
    total = tiles.shape[0]
    index = jnp.arange(total, dtype=jnp.int32)
    split_of = (index // TILES_DEV) % N_SPLIT
    global_col = (split_of * NUBLK + tile_col).astype(jnp.int32)
    global_row = (tile_dest[:, 0] * RBLK + tile_row).astype(jnp.int32)
    dens_blocks = density.reshape(NUBLK * N_SPLIT, B, OCC)
    turns = total // TILES_DEV
    tile_sets = tiles.reshape(turns, TILES_DEV, B, B)
    row_sets = global_row.reshape(turns, TILES_DEV)
    col_sets = global_col.reshape(turns, TILES_DEV)

    def step(acc, packed):
        tile_part, row_part, col_part = packed
        picked = dens_blocks[col_part]
        product = jnp.einsum("sab,sbo->sao", tile_part.astype(jnp.float32), picked.astype(jnp.float32))
        return acc.at[row_part].add(product), None

    acc = jnp.zeros((RBLK * N_ROW, B, OCC), jnp.float32)
    acc, unused = lax.scan(step, acc, (tile_sets, row_sets, col_sets))
    return acc.reshape(RBLK * N_ROW * B, OCC).astype(jnp.bfloat16)
```

```python
import functools

import jax
import jax.numpy as jnp
from jax import lax
from jax.experimental import pallas as pl
from jax.experimental.pallas import tpu as pltpu
from jax.sharding import PartitionSpec as P

MESH = pl.DeviceIdType.MESH
B = 64
LANES = 128
ROWS = B * B // LANES
CAP = 3
NX = 4


def shift(at, by, size):
    return lax.rem(at + by, size)


def kernel(
    n_row, n_split, meta_ref, tiles_ref, dens_ref, out_ref,
    pack, pack_s, send, recv, lab_send, lab_recv, plan, plan_s, sums,
    xsend, xrecv, usend, urecv, dsend, drecv,
    local_sem, lab_ss, lab_rs, tile_ss, tile_rs, x_ss, x_rs, u_ss, u_rs, d_ss, d_rs,
):
    nz, ny = n_row // NX, n_split // 2
    count = tiles_ref.shape[0]
    half = ny // 2
    slots = n_row * CAP
    row, split = lax.axis_index("row"), lax.axis_index("split")
    x, z = row // nz, lax.rem(row, nz)
    y, core = split // 2, lax.rem(split, 2)
    other = (row, y * 2 + 1 - core)
    above = (row, shift(y, 1, ny) * 2 + core)
    below = (row, shift(y, ny - 1, ny) * 2 + core)

    def offset(q):
        u = (n_row - q) % n_row
        k = u // NX
        odd = k % 2
        return u % NX, odd * ((k + 1) // 2) + (1 - odd) * ((nz - k // 2) % nz)

    def owner(q):
        dx, dz = offset(q)
        return (x + dx) % NX * nz + (z + dz) % nz

    barrier = pltpu.get_barrier_semaphore()

    def greet(q, carry):
        pl.semaphore_signal(barrier, inc=1, device_id=(owner(q), split), device_id_type=MESH)
        return carry

    lax.fori_loop(1, n_row, greet, 0)
    for peer in (other, above, below):
        pl.semaphore_signal(barrier, inc=1, device_id=peer, device_id_type=MESH)

    dest = meta_ref[0:1, :]
    label = meta_ref[1:2, :]
    width = dest.shape[1]
    t_sub = lax.broadcasted_iota(jnp.int32, (width, width), 0)
    t_lane = lax.broadcasted_iota(jnp.int32, (width, width), 1)
    dest_col = jnp.sum(jnp.where(t_sub == t_lane, dest, 0), axis=1, keepdims=True)
    rank = jnp.sum(jnp.where((dest_col == dest) & (t_sub < t_lane), 1, 0), axis=0, keepdims=True)
    q_sub = lax.broadcasted_iota(jnp.int32, (n_row, LANES), 0)
    lane = lax.broadcasted_iota(jnp.int32, (n_row, LANES), 1)
    u = jnp.where(q_sub == 0, 0, n_row - q_sub)
    k = u // NX
    dz = jnp.where(k % 2 == 1, (k + 1) // 2, (nz - k // 2) % nz)
    to = (x + u % NX) % NX * nz + (z + dz) % nz
    packed = jnp.zeros((n_row, LANES), jnp.int32)
    for i in range(CAP):
        hit = (to == dest) & (rank == i)
        which = jnp.sum(jnp.where(hit, lane, 0), axis=1, keepdims=True)
        tag = jnp.sum(jnp.where(hit, label, 0), axis=1, keepdims=True)
        packed = jnp.where(lane == i, which, jnp.where(lane == CAP + i, tag, packed))
    pack[...] = packed
    fetch = pltpu.make_async_copy(pack, pack_s, local_sem.at[0])
    fetch.start()

    def set_label(q, carry):
        lab_send[q] = pack[pl.ds(q, 1), :]
        return carry

    lax.fori_loop(0, n_row, set_label, 0)
    lab_recv[0] = lab_send[0]

    pl.semaphore_wait(barrier, n_row - 1 + 3)

    def label_copy(q):
        return pltpu.make_async_remote_copy(
            src_ref=lab_send.at[q], dst_ref=lab_recv.at[q], send_sem=lab_ss.at[q], recv_sem=lab_rs.at[q],
            device_id=(owner(q), split), device_id_type=MESH,
        )

    def tile_copy(q):
        return pltpu.make_async_remote_copy(
            src_ref=send.at[q], dst_ref=recv.at[q], send_sem=tile_ss.at[q], recv_sem=tile_rs.at[q],
            device_id=(owner(q), split), device_id_type=MESH,
        )

    def send_label(q, carry):
        label_copy(q).start()
        return carry

    lax.fori_loop(1, n_row, send_label, 0)
    fetch.wait()

    def send_tiles(q, carry):
        for i in range(CAP):
            send[q, pl.ds(i * ROWS, ROWS), :] = tiles_ref[pack_s[q, i]]
        tile_copy(q).start()
        return carry

    lax.fori_loop(1, n_row, send_tiles, 0)
    for i in range(CAP):
        recv[0, pl.ds(i * ROWS, ROWS), :] = tiles_ref[pack_s[0, i]]

    def wait_label(q, carry):
        label_copy(q).wait_recv()
        return carry

    lax.fori_loop(1, n_row, wait_label, 0)
    for q in range(n_row):
        pack[q:q + 1, :] = lab_recv[q]
    labels = pack[...]
    nothing = slots
    rows_of, cols_of, across = [], [], []
    for i in range(CAP):
        tag = jnp.sum(jnp.where(lane == CAP + i, labels, 0), axis=1, keepdims=True) - 1
        rows_of.append(tag >> 4)
        cols_of.append(tag & 15)
        across.append(jnp.sum(jnp.where(lane == q_sub, rows_of[i], 0), axis=0, keepdims=True))
    planned = jnp.zeros((n_row, LANES), jnp.int32)
    last = jnp.full((n_row, LANES), -1, jnp.int32)
    for i in range(CAP):
        best = jnp.full((n_row, LANES), -1, jnp.int32)
        for h in range(CAP):
            earlier = (lane <= q_sub) if h < i else (lane < q_sub)
            best = jnp.maximum(best, jnp.where(earlier & (rows_of[i] == across[h]), lane * CAP + h, -1))
        before = jnp.max(best, axis=1, keepdims=True)
        before = jnp.where(before < 0, nothing, before)
        planned = jnp.where(lane == i, before, jnp.where(lane == CAP + i, cols_of[i], planned))
        last = jnp.maximum(last, jnp.where(rows_of[i] == lane, q_sub * CAP + i, -1))
    last = jnp.max(last, axis=0, keepdims=True)
    plan[0:n_row, :] = planned
    plan[n_row:n_row + 8, :] = jnp.broadcast_to(jnp.where(last < 0, nothing, last), (8, LANES))
    fetch_plan = pltpu.make_async_copy(plan, plan_s, local_sem.at[1])
    fetch_plan.start()
    sums[nothing] = jnp.zeros((B, sums.shape[2]), jnp.float32)
    fetch_plan.wait()

    def work(q):
        products = []
        for i in range(CAP):
            block = recv[q, pl.ds(i * ROWS, ROWS), :]
            lhs = jnp.concatenate([block[:, :B], block[:, B:]], axis=0)
            products.append(jnp.dot(lhs, dens_ref[plan_s[q, CAP + i]], preferred_element_type=jnp.float32))
        for i in range(CAP):
            sums[q * CAP + i] = products[i] + sums[plan_s[q, i]]

    work(0)

    def turn(q, carry):
        tile_copy(q).wait_recv()
        work(q)
        return carry

    lax.fori_loop(1, n_row, turn, 0)

    def partial(ahead, c, b):
        g = (shift(y, ahead, ny) * 2 + c) * 2 + b
        return sums[plan_s[n_row, g]]

    def x_copy(ahead):
        return pltpu.make_async_remote_copy(
            src_ref=xsend.at[ahead], dst_ref=xrecv.at[ahead], send_sem=x_ss.at[ahead], recv_sem=x_rs.at[ahead],
            device_id=other, device_id_type=MESH,
        )

    order = [half]
    for t in range(1, half):
        order += [half - t, half + t]
    order += [0]
    for ahead in order:
        for b in range(2):
            xsend[ahead, b] = partial(ahead, 1 - core, b)
        x_copy(ahead).start()

    def u_copy(t, b):
        return pltpu.make_async_remote_copy(
            src_ref=usend.at[t, b], dst_ref=urecv.at[t, b], send_sem=u_ss.at[t, b], recv_sem=u_rs.at[t, b],
            device_id=above, device_id_type=MESH,
        )

    def d_copy(t, b):
        return pltpu.make_async_remote_copy(
            src_ref=dsend.at[t, b], dst_ref=drecv.at[t, b], send_sem=d_ss.at[t, b], recv_sem=d_rs.at[t, b],
            device_id=below, device_id_type=MESH,
        )

    def mine(ahead, b):
        return partial(ahead, core, b) + xrecv[ahead, b]

    sent = []
    x_copy(half).wait_recv()
    usend[0, 0] = mine(half, 0)
    u_copy(0, 0).start()
    dsend[0, 1] = mine(half, 1)
    d_copy(0, 1).start()
    sent += [u_copy(0, 0), d_copy(0, 1)]
    for t in range(1, half):
        x_copy(half - t).wait_recv()
        x_copy(half + t).wait_recv()
        for step in range(2):
            b = step
            term = mine(half - t, b)
            if t > 1 or b == 0:
                u_copy(t - 1, b).wait_recv()
                term = term + urecv[t - 1, b]
            usend[t, b] = term
            u_copy(t, b).start()
            b = 1 - step
            term = mine(half + t, b)
            if t > 1 or b == 1:
                d_copy(t - 1, b).wait_recv()
                term = term + drecv[t - 1, b]
            dsend[t, b] = term
            d_copy(t, b).start()
            sent += [u_copy(t, step), d_copy(t, b)]
    x_copy(0).wait_recv()
    to_row = lax.broadcasted_iota(jnp.int32, (B, B), 0)
    from_row = lax.broadcasted_iota(jnp.int32, (B, B), 1)
    swap = (from_row == to_row % 2 * ROWS + to_row // 2).astype(jnp.bfloat16)
    for b in range(2):
        total = mine(0, b)
        if half > 1 or b == 0:
            u_copy(half - 1, b).wait_recv()
            total = total + urecv[half - 1, b]
        if half > 1 or b == 1:
            d_copy(half - 1, b).wait_recv()
            total = total + drecv[half - 1, b]
        rounded = total.astype(jnp.bfloat16)
        out_ref[pl.ds(b * B, B), :] = jnp.dot(
            swap, rounded, preferred_element_type=jnp.float32
        ).astype(jnp.bfloat16)

    def finish(q, carry):
        label_copy(q).wait_send()
        tile_copy(q).wait_send()
        return carry

    lax.fori_loop(1, n_row, finish, 0)
    for ahead in order:
        x_copy(ahead).wait_send()
    for copy in sent:
        copy.wait_send()


def on_device(n_row, n_split, tiles, tile_dest, tile_row, tile_col, density):
    count, orbitals = tiles.shape[0], density.shape[1]
    ny = n_split // 2
    half = ny // 2
    label = 1 + tile_row * 16 + tile_col
    meta = jnp.stack([tile_dest[:, 0], label])
    meta = jnp.pad(meta, ((0, 0), (0, LANES - count)), constant_values=-1)
    blocks = tiles.reshape(count, ROWS, LANES)
    vmem = pl.BlockSpec(memory_space=pltpu.VMEM)
    f32, i32, bf16 = jnp.float32, jnp.int32, jnp.bfloat16
    dma = pltpu.SemaphoreType.DMA
    return pl.pallas_call(
        functools.partial(kernel, n_row, n_split),
        out_shape=jax.ShapeDtypeStruct((2 * B, orbitals), bf16),
        in_specs=[vmem] * 3,
        out_specs=vmem,
        scratch_shapes=[
            pltpu.VMEM((n_row, LANES), i32),
            pltpu.SMEM((n_row, LANES), i32),
            pltpu.VMEM((n_row, CAP * ROWS, LANES), bf16),
            pltpu.VMEM((n_row, CAP * ROWS, LANES), bf16),
            pltpu.VMEM((n_row, 1, LANES), i32),
            pltpu.VMEM((n_row, 1, LANES), i32),
            pltpu.VMEM((n_row + 8, LANES), i32),
            pltpu.SMEM((n_row + 8, LANES), i32),
            pltpu.VMEM((n_row * CAP + 1, B, orbitals), f32),
            pltpu.VMEM((ny, 2, B, orbitals), f32),
            pltpu.VMEM((ny, 2, B, orbitals), f32),
            pltpu.VMEM((half, 2, B, orbitals), f32),
            pltpu.VMEM((half, 2, B, orbitals), f32),
            pltpu.VMEM((half, 2, B, orbitals), f32),
            pltpu.VMEM((half, 2, B, orbitals), f32),
            dma((2,)), dma((n_row,)), dma((n_row,)), dma((n_row,)), dma((n_row,)),
            dma((ny,)), dma((ny,)), dma((half, 2)), dma((half, 2)), dma((half, 2)), dma((half, 2)),
        ],
        compiler_params=pltpu.CompilerParams(
            collective_id=0, has_side_effects=True, vmem_limit_bytes=40 * 2**20
        ),
        cost_estimate=pl.CostEstimate(
            flops=2 * n_row * CAP * B * B * orbitals, bytes_accessed=tiles.size * 2, transcendentals=0
        ),
    )(meta, blocks, density.reshape(-1, B, orbitals))


def solution(mesh):
    n_row, n_split = mesh.shape["row"], mesh.shape["split"]
    placed = (
        P(("row", "split"), None),
        P(("row", "split"), None),
        P(("row", "split")),
        P(("row", "split")),
        P("split", None),
    )
    return jax.shard_map(
        functools.partial(on_device, n_row, n_split),
        mesh=mesh, in_specs=placed, out_specs=P(("row", "split"), None), check_vma=False,
    )
```

```python
import functools

import jax
import jax.numpy as jnp
from jax import lax
from jax.experimental import pallas as pl
from jax.experimental.pallas import tpu as pltpu
from jax.sharding import PartitionSpec as P

MESH = pl.DeviceIdType.MESH
B = 64
LANES = 128
ROWS = B * B // LANES
CAP = 3
NX = 4


def shift(at, by, size):
    return lax.rem(at + by, size)


def kernel(
    n_row, n_split, dest_hbm, row_hbm, col_hbm, tiles_hbm, dens_hbm, out_ref,
    dest_v, row_v, col_v, tiles_v, dens_ref, tall,
    pack, pack_s, send, recv, lab_send, lab_recv, plan, plan_s, sums,
    xsend, xrecv, usend0, urecv0, dsend0, drecv0, usend, urecv, dsend, drecv,
    local_sem, lab_ss, lab_rs, tile_ss, tile_rs, x_ss, x_rs,
    u0_ss, u0_rs, d0_ss, d0_rs, u_ss, u_rs, d_ss, d_rs,
):
    nz, ny = n_row // NX, n_split // 2
    half = ny // 2
    slots = n_row * CAP
    row, split = lax.axis_index("row"), lax.axis_index("split")
    x, z = row // nz, lax.rem(row, nz)
    y, core = split // 2, lax.rem(split, 2)
    up_y, down_y = shift(y, 1, ny) * 2, shift(y, ny - 1, ny) * 2
    other = (row, y * 2 + 1 - core)
    above, above_other = (row, up_y + core), (row, up_y + 1 - core)
    below, below_other = (row, down_y + core), (row, down_y + 1 - core)

    def offset(q):
        u = (n_row - q) % n_row
        k = u // NX
        odd = k % 2
        return u % NX, odd * ((k + 1) // 2) + (1 - odd) * ((nz - k // 2) % nz)

    def owner(q):
        dx, dz = offset(q)
        return (x + dx) % NX * nz + (z + dz) % nz

    fetches = []
    for i, (src, dst) in enumerate(
        [(dest_hbm, dest_v), (row_hbm, row_v), (col_hbm, col_v), (tiles_hbm, tiles_v), (dens_hbm, dens_ref)]
    ):
        fetches.append(pltpu.make_async_copy(src, dst, local_sem.at[2 + i]))
        fetches[i].start()

    barrier = pltpu.get_barrier_semaphore()

    def greet(q, carry):
        pl.semaphore_signal(barrier, inc=1, device_id=(owner(q), split), device_id_type=MESH)
        return carry

    lax.fori_loop(1, n_row, greet, 0)
    for peer in (other, above, above_other, below, below_other):
        pl.semaphore_signal(barrier, inc=1, device_id=peer, device_id_type=MESH)

    for i in range(3):
        fetches[i].wait()
    dest = dest_v[...]
    label = 1 + row_v[...] * 16 + col_v[...]
    width = dest.shape[1]
    t_sub = lax.broadcasted_iota(jnp.int32, (width, width), 0)
    t_lane = lax.broadcasted_iota(jnp.int32, (width, width), 1)
    dest_col = jnp.sum(jnp.where(t_sub == t_lane, dest, 0), axis=1, keepdims=True)
    rank = jnp.sum(jnp.where((dest_col == dest) & (t_sub < t_lane), 1, 0), axis=0, keepdims=True)
    q_sub = lax.broadcasted_iota(jnp.int32, (n_row, LANES), 0)
    lane = lax.broadcasted_iota(jnp.int32, (n_row, LANES), 1)
    t_of = lax.broadcasted_iota(jnp.int32, (n_row, width), 1)
    q_of = lax.broadcasted_iota(jnp.int32, (n_row, 1), 0)
    u = jnp.where(q_of == 0, 0, n_row - q_of)
    k = u // NX
    dz = jnp.where(k % 2 == 1, (k + 1) // 2, (nz - k // 2) % nz)
    to = (x + u % NX) % NX * nz + (z + dz) % nz
    packed = jnp.zeros((n_row, LANES), jnp.int32)
    for i in range(CAP):
        hit = (to == dest) & (rank == i)
        which = jnp.sum(jnp.where(hit, t_of, 0), axis=1, keepdims=True)
        tag = jnp.sum(jnp.where(hit, label, 0), axis=1, keepdims=True)
        packed = jnp.where(lane == i, which, jnp.where(lane == CAP + i, tag, packed))
    pack[...] = packed
    fetch = pltpu.make_async_copy(pack, pack_s, local_sem.at[0])
    fetch.start()

    fetches[3].wait()
    def lay(g, carry):
        group = tiles_v[g].astype(jnp.float32)
        for p in range(ROWS):
            tall[pl.ds(g * 8, 8), p, :] = group[p]
        return carry

    lax.fori_loop(0, tiles_v.shape[0], lay, 0)

    def set_label(q, carry):
        lab_send[q] = pack[pl.ds(q, 1), :]
        return carry

    lax.fori_loop(0, n_row, set_label, 0)
    lab_recv[0] = lab_send[0]
    fetch.wait()

    pl.semaphore_wait(barrier, n_row - 1 + 5)

    def label_copy(q):
        return pltpu.make_async_remote_copy(
            src_ref=lab_send.at[q], dst_ref=lab_recv.at[q], send_sem=lab_ss.at[q], recv_sem=lab_rs.at[q],
            device_id=(owner(q), split), device_id_type=MESH,
        )

    def tile_copy(q):
        return pltpu.make_async_remote_copy(
            src_ref=send.at[q], dst_ref=recv.at[q], send_sem=tile_ss.at[q], recv_sem=tile_rs.at[q],
            device_id=(owner(q), split), device_id_type=MESH,
        )

    def send_label(q, carry):
        label_copy(q).start()
        return carry

    def send_tiles(q, carry):
        for i in range(CAP):
            send[q, pl.ds(i * ROWS, ROWS), :] = tall[pack_s[q, i]].astype(jnp.bfloat16)
        tile_copy(q).start()
        return carry

    ahead_of_labels = min(9, n_row)
    lax.fori_loop(1, ahead_of_labels, send_tiles, 0)
    lax.fori_loop(1, n_row, send_label, 0)
    lax.fori_loop(ahead_of_labels, n_row, send_tiles, 0)
    for i in range(CAP):
        recv[0, pl.ds(i * ROWS, ROWS), :] = tall[pack_s[0, i]].astype(jnp.bfloat16)

    def wait_label(q, carry):
        label_copy(q).wait_recv()
        return carry

    lax.fori_loop(1, n_row, wait_label, 0)
    for q in range(n_row):
        pack[q:q + 1, :] = lab_recv[q]
    labels = pack[...]
    nothing = slots
    rows_of, cols_of, across = [], [], []
    for i in range(CAP):
        tag = jnp.sum(jnp.where(lane == CAP + i, labels, 0), axis=1, keepdims=True) - 1
        rows_of.append(tag >> 4)
        cols_of.append(tag & 15)
        across.append(jnp.sum(jnp.where(lane == q_sub, rows_of[i], 0), axis=0, keepdims=True))
    planned = jnp.zeros((n_row, LANES), jnp.int32)
    last = jnp.full((n_row, LANES), -1, jnp.int32)
    for i in range(CAP):
        best = jnp.full((n_row, LANES), -1, jnp.int32)
        for h in range(CAP):
            earlier = (lane <= q_sub) if h < i else (lane < q_sub)
            best = jnp.maximum(best, jnp.where(earlier & (rows_of[i] == across[h]), lane * CAP + h, -1))
        before = jnp.max(best, axis=1, keepdims=True)
        before = jnp.where(before < 0, nothing, before)
        planned = jnp.where(lane == i, before, jnp.where(lane == CAP + i, cols_of[i], planned))
        last = jnp.maximum(last, jnp.where(rows_of[i] == lane, q_sub * CAP + i, -1))
    last = jnp.max(last, axis=0, keepdims=True)
    plan[0:n_row, :] = planned
    plan[n_row:n_row + 8, :] = jnp.broadcast_to(jnp.where(last < 0, nothing, last), (8, LANES))
    fetch_plan = pltpu.make_async_copy(plan, plan_s, local_sem.at[1])
    fetch_plan.start()
    sums[nothing] = jnp.zeros((B, sums.shape[2]), jnp.float32)
    fetch_plan.wait()
    fetches[4].wait()

    def work(q):
        products = []
        for i in range(CAP):
            block = recv[q, pl.ds(i * ROWS, ROWS), :]
            lhs = jnp.concatenate([block[:, :B], block[:, B:]], axis=0)
            products.append(jnp.dot(lhs, dens_ref[plan_s[q, CAP + i]], preferred_element_type=jnp.float32))
        for i in range(CAP):
            sums[q * CAP + i] = products[i] + sums[plan_s[q, i]]

    work(0)

    def turn(q, carry):
        tile_copy(q).wait_recv()
        work(q)
        return carry

    lax.fori_loop(1, n_row, turn, 0)

    def partial(ahead, c, b):
        g = (shift(y, ahead, ny) * 2 + c) * 2 + b
        return sums[plan_s[n_row, g]]

    def remote(src, dst, ss, rs, to):
        return pltpu.make_async_remote_copy(
            src_ref=src, dst_ref=dst, send_sem=ss, recv_sem=rs, device_id=to, device_id_type=MESH
        )

    def first(way, c, h):
        if way == 0:
            return remote(usend0.at[c, h], urecv0.at[c, h], u0_ss.at[c, h], u0_rs.at[c, h], (above, above_other)[c])
        return remote(dsend0.at[c, h], drecv0.at[c, h], d0_ss.at[c, h], d0_rs.at[c, h], (below, below_other)[c])

    def later(way, t, b, h):
        if way == 0:
            return remote(usend.at[t, b, h], urecv.at[t, b, h], u_ss.at[t, b, h], u_rs.at[t, b, h], above)
        return remote(dsend.at[t, b, h], drecv.at[t, b, h], d_ss.at[t, b, h], d_rs.at[t, b, h], below)

    def x_copy(ahead):
        return remote(xsend.at[ahead], xrecv.at[ahead], x_ss.at[ahead], x_rs.at[ahead], other)

    sent = []

    def go(copy):
        copy.start()
        sent.append(copy)

    for c in range(2):
        shares = [partial(half, (core, 1 - core)[c], way) for way in range(2)]
        for h in range(2):
            for way in range(2):
                (usend0, dsend0)[way][c, h] = shares[way][h * ROWS:(h + 1) * ROWS]
                go(first(way, c, h))
    order = []
    for t in range(1, half):
        order += [half - t, half + t]
    order += [0]
    for ahead in order:
        for b in range(2):
            xsend[ahead, b] = partial(ahead, 1 - core, b)
        go(x_copy(ahead))

    def finish(q, carry):
        label_copy(q).wait_send()
        tile_copy(q).wait_send()
        return carry

    lax.fori_loop(1, n_row, finish, 0)

    def came(way, t, b, h):
        if t == 0:
            if way != b:
                return 0.0
            got = 0.0
            for c in range(2):
                first(way, c, h).wait_recv()
                got = got + (urecv0, drecv0)[way][c, h]
            return got
        later(way, t, b, h).wait_recv()
        return (urecv, drecv)[way][t, b, h]

    for t in range(1, half):
        x_copy(half - t).wait_recv()
        x_copy(half + t).wait_recv()
        for step in range(2):
            for way, b in ((0, 1 - step), (1, step)):
                ahead = half - t if way == 0 else half + t
                term = partial(ahead, core, b) + xrecv[ahead, b]
                for h in range(2):
                    (usend, dsend)[way][t, b, h] = term[h * ROWS:(h + 1) * ROWS] + came(way, t - 1, b, h)
                    go(later(way, t, b, h))
    x_copy(0).wait_recv()
    to_row = lax.broadcasted_iota(jnp.int32, (B, B), 0)
    from_row = lax.broadcasted_iota(jnp.int32, (B, B), 1)
    swap = (from_row == to_row % 2 * ROWS + to_row // 2).astype(jnp.bfloat16)
    for b in range(2):
        term = partial(0, core, b) + xrecv[0, b]
        halves = []
        for h in range(2):
            total = term[h * ROWS:(h + 1) * ROWS] + came(0, half - 1, b, h) + came(1, half - 1, b, h)
            halves.append(total.astype(jnp.bfloat16))
        out_ref[pl.ds(b * B, B), :] = jnp.dot(
            swap, jnp.concatenate(halves, axis=0), preferred_element_type=jnp.float32
        ).astype(jnp.bfloat16)
    for copy in sent:
        copy.wait_send()


def on_device(n_row, n_split, tiles, tile_dest, tile_row, tile_col, density):
    count, orbitals = tiles.shape[0], density.shape[1]
    ny = n_split // 2
    half = ny // 2
    groups = tiles.reshape(count // 8, 8, ROWS, LANES).transpose(0, 2, 1, 3)
    vmem = pl.BlockSpec(memory_space=pltpu.VMEM)
    hbm = pl.BlockSpec(memory_space=pltpu.HBM)
    f32, i32, bf16 = jnp.float32, jnp.int32, jnp.bfloat16
    dma = pltpu.SemaphoreType.DMA
    return pl.pallas_call(
        functools.partial(kernel, n_row, n_split),
        out_shape=jax.ShapeDtypeStruct((2 * B, orbitals), bf16),
        in_specs=[hbm] * 5,
        out_specs=vmem,
        scratch_shapes=[
            pltpu.VMEM((1, count), i32),
            pltpu.VMEM((1, count), i32),
            pltpu.VMEM((1, count), i32),
            pltpu.VMEM(groups.shape, bf16),
            pltpu.VMEM((density.shape[0] // B, B, orbitals), bf16),
            pltpu.VMEM((count, ROWS, LANES), f32),
            pltpu.VMEM((n_row, LANES), i32),
            pltpu.SMEM((n_row, LANES), i32),
            pltpu.VMEM((n_row, CAP * ROWS, LANES), bf16),
            pltpu.VMEM((n_row, CAP * ROWS, LANES), bf16),
            pltpu.VMEM((n_row, 1, LANES), i32),
            pltpu.VMEM((n_row, 1, LANES), i32),
            pltpu.VMEM((n_row + 8, LANES), i32),
            pltpu.SMEM((n_row + 8, LANES), i32),
            pltpu.VMEM((n_row * CAP + 1, B, orbitals), f32),
            pltpu.VMEM((ny, 2, B, orbitals), f32),
            pltpu.VMEM((ny, 2, B, orbitals), f32),
            *[pltpu.VMEM((2, 2, ROWS, orbitals), f32)] * 4,
            *[pltpu.VMEM((half, 2, 2, ROWS, orbitals), f32)] * 4,
            dma((7,)), *[dma((n_row,))] * 4, *[dma((ny,))] * 2, *[dma((2, 2))] * 4, *[dma((half, 2, 2))] * 4,
        ],
        compiler_params=pltpu.CompilerParams(
            collective_id=0, has_side_effects=True, vmem_limit_bytes=63 * 2**20
        ),
        cost_estimate=pl.CostEstimate(
            flops=2 * n_row * CAP * B * B * orbitals, bytes_accessed=tiles.size * 2, transcendentals=0
        ),
    )(
        tile_dest.reshape(1, count), tile_row.reshape(1, count), tile_col.reshape(1, count), groups,
        density.reshape(-1, B, orbitals),
    )


def solution(mesh):
    n_row, n_split = mesh.shape["row"], mesh.shape["split"]
    placed = (
        P(("row", "split"), None),
        P(("row", "split"), None),
        P(("row", "split")),
        P(("row", "split")),
        P("split", None),
    )
    return jax.shard_map(
        functools.partial(on_device, n_row, n_split),
        mesh=mesh, in_specs=placed, out_specs=P(("row", "split"), None), check_vma=False,
    )
```

```python
import functools

import jax
import jax.numpy as jnp
from jax import lax
from jax.experimental import pallas as pl
from jax.experimental.pallas import tpu as pltpu
from jax.sharding import PartitionSpec as P

MESH = pl.DeviceIdType.MESH
B = 64
LANES = 128
ROWS = B * B // LANES
CAP = 3
NX = 4


def shift(at, by, size):
    return lax.rem(at + by, size)


def kernel(
    n_row, n_split, dest_hbm, row_hbm, col_hbm, tiles_hbm, dens_hbm, out_ref,
    dest_v, row_v, col_v, tiles_v, dens_ref, tall,
    pack, pack_s, send, recv, lab_send, lab_recv, plan, plan_s, sums,
    xsend, xrecv, first_send, first_recv, later_send, later_recv, back_send, back_recv,
    local_sem, lab_ss, lab_rs, tile_ss, tile_rs, x_ss, x_rs,
    first_ss, first_rs, later_ss, later_rs, back_ss, back_rs,
):
    nz, ny = n_row // NX, n_split // 2
    half, opposite = ny // 2, nz // 2
    places = n_row // 2
    row, split = lax.axis_index("row"), lax.axis_index("split")
    x, z = row // nz, lax.rem(row, nz)
    y, core = split // 2, lax.rem(split, 2)
    up_y, down_y = shift(y, 1, ny) * 2, shift(y, ny - 1, ny) * 2
    other = (row, y * 2 + 1 - core)
    above, above_other = (row, up_y + core), (row, up_y + 1 - core)
    below, below_other = (row, down_y + core), (row, down_y + 1 - core)

    def at_row(dx, dz):
        return shift(x, dx, NX) * nz + shift(z, dz, nz)

    def place(q, x_of, z_of):
        u = (places - q) % places
        k = u // NX
        odd = k % 2
        px = (x_of + u % NX) % NX
        dz = odd * ((k + 1) // 2) + (1 - odd) * (nz - k // 2)
        flip = (k // (opposite - 1)) * (px % 2) if opposite > 1 else 0
        dz = dz + flip * (nz - 2 * dz)
        return px, (z_of + dz) % nz

    def device(q):
        px, pz = place(q, x, z)
        return px * nz + pz, split

    fetches = []
    for i, (src, dst) in enumerate(
        [(dest_hbm, dest_v), (row_hbm, row_v), (col_hbm, col_v), (tiles_hbm, tiles_v), (dens_hbm, dens_ref)]
    ):
        fetches.append(pltpu.make_async_copy(src, dst, local_sem.at[2 + i]))
        fetches[i].start()

    barrier = pltpu.get_barrier_semaphore()
    reach = opposite // 2
    near = {(dx, dz % nz) for dx in range(NX) for dz in range(-reach, reach + 1)} | {(0, opposite)}
    near = sorted(near - {(0, 0)})
    for dx, dz in near:
        pl.semaphore_signal(barrier, inc=1, device_id=(at_row(dx, dz), split), device_id_type=MESH)
    for peer in (other, above, above_other, below, below_other):
        pl.semaphore_signal(barrier, inc=1, device_id=peer, device_id_type=MESH)

    for i in range(3):
        fetches[i].wait()
    dest = dest_v[...]
    label = 1 + row_v[...] * 16 + col_v[...]
    width = dest.shape[1]
    t_sub = lax.broadcasted_iota(jnp.int32, (width, width), 0)
    t_lane = lax.broadcasted_iota(jnp.int32, (width, width), 1)
    dest_col = jnp.sum(jnp.where(t_sub == t_lane, dest, 0), axis=1, keepdims=True)
    rank = jnp.sum(jnp.where((dest_col == dest) & (t_sub < t_lane), 1, 0), axis=0, keepdims=True)
    q_sub = lax.broadcasted_iota(jnp.int32, (places, LANES), 0)
    lane = lax.broadcasted_iota(jnp.int32, (places, LANES), 1)
    t_of = lax.broadcasted_iota(jnp.int32, (places, width), 1)
    q_of = lax.broadcasted_iota(jnp.int32, (places, 1), 0)
    px, pz = place(q_of, x, z)
    packed = jnp.zeros((places, LANES), jnp.int32)
    for i in range(2 * CAP):
        to = px * nz + ((pz + opposite) % nz if i < CAP else pz)
        hit = (to == dest) & (rank == i % CAP)
        which = jnp.sum(jnp.where(hit, t_of, 0), axis=1, keepdims=True)
        tag = jnp.sum(jnp.where(hit, label, 0), axis=1, keepdims=True)
        packed = jnp.where(lane == i, which, jnp.where(lane == 2 * CAP + i, tag, packed))
    pack[...] = packed
    fetch = pltpu.make_async_copy(pack, pack_s, local_sem.at[0])
    fetch.start()

    fetches[3].wait()

    def lay(g, carry):
        group = tiles_v[g].astype(jnp.float32)
        for p in range(ROWS):
            tall[pl.ds(g * 8, 8), p, :] = group[p]
        return carry

    lax.fori_loop(0, tiles_v.shape[0], lay, 0)

    def set_label(q, carry):
        lab_send[q] = pack[pl.ds(q, 1), :]
        return carry

    lax.fori_loop(0, places, set_label, 0)
    lab_recv[0] = lab_send[0]
    fetch.wait()

    pl.semaphore_wait(barrier, len(near) + 5)

    def remote(src, dst, ss, rs, to):
        return pltpu.make_async_remote_copy(
            src_ref=src, dst_ref=dst, send_sem=ss, recv_sem=rs, device_id=to, device_id_type=MESH
        )

    def label_copy(q):
        return remote(lab_send.at[q], lab_recv.at[q], lab_ss.at[q], lab_rs.at[q], device(q))

    def tile_copy(part, q):
        return remote(send.at[part, q], recv.at[part, q], tile_ss.at[part, q], tile_rs.at[part, q], device(q))

    def send_label(q, carry):
        label_copy(q).start()
        return carry

    def blocks_to(ref, part, q):
        for i in range(CAP):
            ref[part, q, pl.ds(i * ROWS, ROWS), :] = tall[pack_s[q, part * CAP + i]].astype(jnp.bfloat16)

    def send_tiles(part):
        def step(q, carry):
            blocks_to(send, part, q)
            tile_copy(part, q).start()
            return carry
        return step

    ahead_of_labels = min(9, places)
    lax.fori_loop(1, ahead_of_labels, send_tiles(0), 0)
    lax.fori_loop(1, places, send_label, 0)
    lax.fori_loop(ahead_of_labels, places, send_tiles(0), 0)
    for part in range(2):
        blocks_to(recv, part, 0)

    def wait_label(q, carry):
        label_copy(q).wait_recv()
        return carry

    lax.fori_loop(1, places, wait_label, 0)
    for q in range(places):
        pack[q:q + 1, :] = lab_recv[q]
    labels = pack[...]
    nothing = 2 * places * CAP
    planned = jnp.zeros((places, LANES), jnp.int32)
    last = jnp.full((places, LANES), -1, jnp.int32)
    for part in range(2):
        rows_of, cols_of, across = [], [], []
        for i in range(CAP):
            tag = jnp.sum(jnp.where(lane == (2 + part) * CAP + i, labels, 0), axis=1, keepdims=True) - 1
            rows_of.append(tag >> 4)
            cols_of.append(tag & 15)
            across.append(jnp.sum(jnp.where(lane == q_sub, rows_of[i], 0), axis=0, keepdims=True))
        base = part * places * CAP
        for i in range(CAP):
            best = jnp.full((places, LANES), -1, jnp.int32)
            for h in range(CAP):
                earlier = (lane <= q_sub) if h < i else (lane < q_sub)
                best = jnp.maximum(best, jnp.where(earlier & (rows_of[i] == across[h]), base + lane * CAP + h, -1))
            before = jnp.max(best, axis=1, keepdims=True)
            before = jnp.where(before < 0, nothing, before)
            at = part * CAP + i
            planned = jnp.where(lane == at, before, jnp.where(lane == 2 * CAP + at, cols_of[i], planned))
            here = (rows_of[i] >= 0) & (rows_of[i] + part * 2 * n_split == lane)
            last = jnp.maximum(last, jnp.where(here, base + q_sub * CAP + i, -1))
    last = jnp.max(last, axis=0, keepdims=True)
    plan[0:places, :] = planned
    plan[places:places + 8, :] = jnp.broadcast_to(jnp.where(last < 0, nothing, last), (8, LANES))
    fetch_plan = pltpu.make_async_copy(plan, plan_s, local_sem.at[1])
    fetch_plan.start()
    sums[nothing] = jnp.zeros((B, sums.shape[2]), jnp.float32)
    fetch_plan.wait()
    fetches[4].wait()

    def work(part, q):
        products = []
        for i in range(CAP):
            block = recv[part, q, pl.ds(i * ROWS, ROWS), :]
            lhs = jnp.concatenate([block[:, :B], block[:, B:]], axis=0)
            col = plan_s[q, (2 + part) * CAP + i]
            products.append(jnp.dot(lhs, dens_ref[col], preferred_element_type=jnp.float32))
        for i in range(CAP):
            sums[(part * places + q) * CAP + i] = products[i] + sums[plan_s[q, part * CAP + i]]

    def turns(part, start, stop):
        def turn(q, carry):
            tile_copy(part, q).wait_recv()
            work(part, q)
            if part == 0:
                send_tiles(1)(q, 0)
            return carry

        if start == 0:
            work(part, 0)
        lax.fori_loop(max(start, 1), stop, turn, 0)

    sent = []

    def go(copy):
        copy.start()
        sent.append(copy)

    order = []
    for t in range(1, half):
        order += [half - t, half + t]
    order += [0]

    def partial(part, ahead, c, b):
        g = (shift(y, ahead, ny) * 2 + c) * 2 + b
        return sums[plan_s[places, part * 2 * n_split + g]]

    def first(part, way, c, h):
        at = (part, way, c, h)
        to = ((above, above_other), (below, below_other))[way][c]
        return remote(first_send.at[at], first_recv.at[at], first_ss.at[at], first_rs.at[at], to)

    def later(part, way, t, b, h):
        at = (part, way, t, b, h)
        return remote(later_send.at[at], later_recv.at[at], later_ss.at[at], later_rs.at[at], (above, below)[way])

    def x_copy(part, ahead):
        at = (part, ahead)
        return remote(xsend.at[at], xrecv.at[at], x_ss.at[at], x_rs.at[at], other)

    def begin(part):
        for c in range(2):
            shares = [partial(part, half, (core, 1 - core)[c], way) for way in range(2)]
            for h in range(2):
                for way in range(2):
                    first_send[part, way, c, h] = shares[way][h * ROWS:(h + 1) * ROWS]
                    go(first(part, way, c, h))
        for ahead in order:
            for b in range(2):
                xsend[part, ahead, b] = partial(part, ahead, 1 - core, b)
            go(x_copy(part, ahead))

    def came(part, way, t, b, h):
        if t == 0:
            if way != b:
                return 0.0
            got = 0.0
            for c in range(2):
                first(part, way, c, h).wait_recv()
                got = got + first_recv[part, way, c, h]
            return got
        later(part, way, t, b, h).wait_recv()
        return later_recv[part, way, t, b, h]

    def forward(part, t):
        x_copy(part, half - t).wait_recv()
        x_copy(part, half + t).wait_recv()
        for step in range(2):
            for way, b in ((0, 1 - step), (1, step)):
                ahead = half - t if way == 0 else half + t
                term = partial(part, ahead, core, b) + xrecv[part, ahead, b]
                for h in range(2):
                    later_send[part, way, t, b, h] = term[h * ROWS:(h + 1) * ROWS] + came(part, way, t - 1, b, h)
                    go(later(part, way, t, b, h))

    def total(part, b, h):
        if b == 0 and h == 0:
            x_copy(part, 0).wait_recv()
        term = partial(part, 0, core, b) + xrecv[part, 0, b]
        return term[h * ROWS:(h + 1) * ROWS] + came(part, 0, half - 1, b, h) + came(part, 1, half - 1, b, h)

    def back(b, h):
        at = (b, h)
        return remote(back_send.at[at], back_recv.at[at], back_ss.at[at], back_rs.at[at], (at_row(0, opposite), split))

    turns(0, 0, places)
    begin(0)
    cuts = [places * i // half for i in range(half + 1)]
    for t in range(half):
        if t > 0:
            forward(0, t)
        turns(1, cuts[t], cuts[t + 1])
    begin(1)
    for b in range(2):
        for h in range(2):
            back_send[b, h] = total(0, b, h)
            go(back(b, h))
    for t in range(1, half):
        forward(1, t)

    def finish(q, carry):
        label_copy(q).wait_send()
        for part in range(2):
            tile_copy(part, q).wait_send()
        return carry

    lax.fori_loop(1, places, finish, 0)
    to_row = lax.broadcasted_iota(jnp.int32, (B, B), 0)
    from_row = lax.broadcasted_iota(jnp.int32, (B, B), 1)
    swap = (from_row == to_row % 2 * ROWS + to_row // 2).astype(jnp.bfloat16)
    for b in range(2):
        halves = []
        for h in range(2):
            whole = total(1, b, h)
            back(b, h).wait_recv()
            halves.append((whole + back_recv[b, h]).astype(jnp.bfloat16))
        out_ref[pl.ds(b * B, B), :] = jnp.dot(
            swap, jnp.concatenate(halves, axis=0), preferred_element_type=jnp.float32
        ).astype(jnp.bfloat16)
    for copy in sent:
        copy.wait_send()


def on_device(n_row, n_split, tiles, tile_dest, tile_row, tile_col, density):
    count, orbitals = tiles.shape[0], density.shape[1]
    places, ny = n_row // 2, n_split // 2
    half = ny // 2
    groups = tiles.reshape(count // 8, 8, ROWS, LANES).transpose(0, 2, 1, 3)
    hbm = pl.BlockSpec(memory_space=pltpu.HBM)
    f32, i32, bf16 = jnp.float32, jnp.int32, jnp.bfloat16
    vmem, smem, dma = pltpu.VMEM, pltpu.SMEM, pltpu.SemaphoreType.DMA
    return pl.pallas_call(
        functools.partial(kernel, n_row, n_split),
        out_shape=jax.ShapeDtypeStruct((2 * B, orbitals), bf16),
        in_specs=[hbm] * 5,
        out_specs=pl.BlockSpec(memory_space=vmem),
        scratch_shapes=[
            *[vmem((1, count), i32)] * 3,
            vmem(groups.shape, bf16),
            vmem((density.shape[0] // B, B, orbitals), bf16),
            vmem((count, ROWS, LANES), f32),
            vmem((places, LANES), i32),
            smem((places, LANES), i32),
            *[vmem((2, places, CAP * ROWS, LANES), bf16)] * 2,
            *[vmem((places, 1, LANES), i32)] * 2,
            vmem((places + 8, LANES), i32),
            smem((places + 8, LANES), i32),
            vmem((2 * places * CAP + 1, B, orbitals), f32),
            *[vmem((2, ny, 2, B, orbitals), f32)] * 2,
            *[vmem((2, 2, 2, 2, ROWS, orbitals), f32)] * 2,
            *[vmem((2, 2, half, 2, 2, ROWS, orbitals), f32)] * 2,
            *[vmem((2, 2, ROWS, orbitals), f32)] * 2,
            dma((7,)), *[dma((places,))] * 2, *[dma((2, places))] * 2, *[dma((2, ny))] * 2,
            *[dma((2, 2, 2, 2))] * 2, *[dma((2, 2, half, 2, 2))] * 2, *[dma((2, 2))] * 2,
        ],
        compiler_params=pltpu.CompilerParams(
            collective_id=0, has_side_effects=True, vmem_limit_bytes=63 * 2**20
        ),
        cost_estimate=pl.CostEstimate(
            flops=2 * n_row * CAP * B * B * orbitals, bytes_accessed=tiles.size * 2, transcendentals=0
        ),
    )(
        tile_dest.reshape(1, count), tile_row.reshape(1, count), tile_col.reshape(1, count), groups,
        density.reshape(-1, B, orbitals),
    )


def solution(mesh):
    n_row, n_split = mesh.shape["row"], mesh.shape["split"]
    placed = (
        P(("row", "split"), None),
        P(("row", "split"), None),
        P(("row", "split")),
        P(("row", "split")),
        P("split", None),
    )
    return jax.shard_map(
        functools.partial(on_device, n_row, n_split),
        mesh=mesh, in_specs=placed, out_specs=P(("row", "split"), None), check_vma=False,
    )
```

```python
import functools

import jax
import jax.numpy as jnp
from jax import lax
from jax.experimental import pallas as pl
from jax.experimental.pallas import tpu as pltpu
from jax.sharding import PartitionSpec as P

MESH = pl.DeviceIdType.MESH
B = 64
LANES = 128
ROWS = B * B // LANES
CAP = 3
NX = 4
PARTS = 1
PIECE = B // PARTS
TOGETHER = 4


def shift(at, by, size):
    return lax.rem(at + by, size)


def kernel(
    n_row, n_split, dest_hbm, row_hbm, col_hbm, tiles_hbm, dens_hbm, out_ref,
    dest_v, row_v, col_v, tiles_v, dens_ref, tall,
    pack, pack_s, send, recv, lab_send, lab_recv, plan, plan_s, sums,
    xsend, xrecv, first_send, first_recv, later_send, later_recv, back_send, back_recv,
    local_sem, lab_ss, lab_rs, tile_ss, tile_rs, x_ss, x_rs,
    first_ss, first_rs, later_ss, later_rs, back_ss, back_rs,
):
    nz, ny = n_row // NX, n_split // 2
    half, opposite = ny // 2, nz // 2
    places = n_row // 2
    row, split = lax.axis_index("row"), lax.axis_index("split")
    x, z = lax.div(row, nz), lax.rem(row, nz)
    y, core = lax.div(split, 2), lax.rem(split, 2)
    up_y, down_y = shift(y, 1, ny) * 2, shift(y, ny - 1, ny) * 2
    other = (row, y * 2 + 1 - core)
    above, above_other = (row, up_y + core), (row, up_y + 1 - core)
    below, below_other = (row, down_y + core), (row, down_y + 1 - core)

    def at_row(dx, dz):
        return shift(x, dx, NX) * nz + shift(z, dz, nz)

    def place(q, x_of, z_of):
        u = lax.rem(places - q, places)
        k = lax.div(u, NX)
        odd = lax.rem(k, 2)
        px = lax.rem(x_of + lax.rem(u, NX), NX)
        dz = odd * lax.div(k + 1, 2) + (1 - odd) * (nz - lax.div(k, 2))
        flip = lax.div(k, opposite - 1) * lax.rem(px, 2) if opposite > 1 else 0
        dz = dz + flip * (nz - 2 * dz)
        return px, lax.rem(z_of + dz, nz)

    def device(q):
        px, pz = place(q, x, z)
        return px * nz + pz, split

    fetches = []
    for i, (src, dst) in enumerate(
        [(dest_hbm, dest_v), (row_hbm, row_v), (col_hbm, col_v), (tiles_hbm, tiles_v), (dens_hbm, dens_ref)]
    ):
        fetches.append(pltpu.make_async_copy(src, dst, local_sem.at[2 + i]))
        fetches[i].start()

    barrier = pltpu.get_barrier_semaphore()
    reach = opposite // 2
    near = {(dx, dz % nz) for dx in range(NX) for dz in range(-reach, reach + 1)} | {(0, opposite)}
    near = sorted(near - {(0, 0)})
    for dx, dz in near:
        pl.semaphore_signal(barrier, inc=1, device_id=(at_row(dx, dz), split), device_id_type=MESH)
    for peer in (other, above, above_other, below, below_other):
        pl.semaphore_signal(barrier, inc=1, device_id=peer, device_id_type=MESH)

    for i in range(3):
        fetches[i].wait()
    dest = dest_v[...]
    label = 1 + row_v[...] * 16 + col_v[...]
    width = dest.shape[1]
    t_sub = lax.broadcasted_iota(jnp.int32, (width, width), 0)
    t_lane = lax.broadcasted_iota(jnp.int32, (width, width), 1)
    dest_col = jnp.sum(jnp.where(t_sub == t_lane, dest, 0), axis=1, keepdims=True)
    rank = jnp.sum(jnp.where((dest_col == dest) & (t_sub < t_lane), 1, 0), axis=0, keepdims=True)
    q_sub = lax.broadcasted_iota(jnp.int32, (places, LANES), 0)
    lane = lax.broadcasted_iota(jnp.int32, (places, LANES), 1)
    t_of = lax.broadcasted_iota(jnp.int32, (places, width), 1)
    q_of = lax.broadcasted_iota(jnp.int32, (places, 1), 0)
    px, pz = place(q_of, x, z)
    packed = jnp.zeros((places, LANES), jnp.int32)
    for i in range(2 * CAP):
        to = px * nz + (lax.rem(pz + opposite, nz) if i < CAP else pz)
        hit = (to == dest) & (rank == i % CAP)
        which = jnp.sum(jnp.where(hit, t_of, 0), axis=1, keepdims=True)
        tag = jnp.sum(jnp.where(hit, label, 0), axis=1, keepdims=True)
        packed = jnp.where(lane == i, which, jnp.where(lane == 2 * CAP + i, tag, packed))
    pack[...] = packed
    fetch = pltpu.make_async_copy(pack, pack_s, local_sem.at[0])
    fetch.start()

    fetches[3].wait()

    def lay(g, carry):
        group = tiles_v[g].astype(jnp.float32)
        for p in range(ROWS):
            tall[pl.ds(g * 8, 8), p, :] = group[p]
        return carry

    lax.fori_loop(0, tiles_v.shape[0], lay, 0)

    def set_label(q, carry):
        lab_send[q] = pack[pl.ds(q, 1), :]
        return carry

    lax.fori_loop(0, places, set_label, 0)
    lab_recv[0] = lab_send[0]
    fetch.wait()

    pl.semaphore_wait(barrier, len(near) + 5)

    def remote(src, dst, ss, rs, to):
        return pltpu.make_async_remote_copy(
            src_ref=src, dst_ref=dst, send_sem=ss, recv_sem=rs, device_id=to, device_id_type=MESH
        )

    def label_copy(q):
        return remote(lab_send.at[q], lab_recv.at[q], lab_ss.at[q], lab_rs.at[q], device(q))

    def tile_copy(part, q):
        return remote(send.at[part, q], recv.at[part, q], tile_ss.at[part, q], tile_rs.at[part, q], device(q))

    def send_label(q, carry):
        label_copy(q).start()
        return carry

    def blocks_to(ref, part, q):
        for i in range(CAP):
            ref[part, q, pl.ds(i * ROWS, ROWS), :] = tall[pack_s[q, part * CAP + i]].astype(jnp.bfloat16)

    def send_tiles(part):
        def step(q, carry):
            blocks_to(send, part, q)
            tile_copy(part, q).start()
            return carry
        return step

    lax.fori_loop(1, places, send_label, 0)
    lax.fori_loop(1, places, send_tiles(0), 0)
    for part in range(2):
        blocks_to(recv, part, 0)

    def wait_label(q, carry):
        label_copy(q).wait_recv()
        return carry

    lax.fori_loop(1, places, wait_label, 0)
    for q in range(places):
        pack[q:q + 1, :] = lab_recv[q]
    labels = pack[...]
    nothing = 2 * places * CAP
    planned = jnp.zeros((places, LANES), jnp.int32)
    last = jnp.full((places, LANES), -1, jnp.int32)
    for part in range(2):
        rows_of, cols_of, across = [], [], []
        for i in range(CAP):
            tag = jnp.sum(jnp.where(lane == (2 + part) * CAP + i, labels, 0), axis=1, keepdims=True) - 1
            rows_of.append(tag >> 4)
            cols_of.append(tag & 15)
            across.append(jnp.sum(jnp.where(lane == q_sub, rows_of[i], 0), axis=0, keepdims=True))
        base = part * places * CAP
        for i in range(CAP):
            best = jnp.full((places, LANES), -1, jnp.int32)
            for h in range(CAP):
                earlier = (lane <= q_sub) if h < i else (lane < q_sub)
                best = jnp.maximum(best, jnp.where(earlier & (rows_of[i] == across[h]), base + lane * CAP + h, -1))
            before = jnp.max(best, axis=1, keepdims=True)
            before = jnp.where(before < 0, nothing, before)
            at = part * CAP + i
            planned = jnp.where(lane == at, before, jnp.where(lane == 2 * CAP + at, cols_of[i], planned))
            here = (rows_of[i] >= 0) & (rows_of[i] + part * 2 * n_split == lane)
            last = jnp.maximum(last, jnp.where(here, base + q_sub * CAP + i, -1))
    last = jnp.max(last, axis=0, keepdims=True)
    plan[0:places, :] = planned
    plan[places:places + 8, :] = jnp.broadcast_to(jnp.where(last < 0, nothing, last), (8, LANES))
    fetch_plan = pltpu.make_async_copy(plan, plan_s, local_sem.at[1])
    fetch_plan.start()
    sums[nothing] = jnp.zeros((B, sums.shape[2]), jnp.float32)
    fetch_plan.wait()
    fetches[4].wait()

    def work(part, q0):
        for j in range(TOGETHER):
            for i in range(CAP):
                block = recv[part, q0 + j, pl.ds(i * ROWS, ROWS), :]
                lhs = jnp.concatenate([block[:, :B], block[:, B:]], axis=0)
                col = plan_s[q0 + j, (2 + part) * CAP + i]
                sums[(part * places + q0 + j) * CAP + i] = jnp.dot(
                    lhs, dens_ref[col], preferred_element_type=jnp.float32
                )
        for j in range(TOGETHER):
            for i in range(CAP):
                at = (part * places + q0 + j) * CAP + i
                sums[at] = sums[at] + sums[plan_s[q0 + j, part * CAP + i]]

    def turns(part, start, stop):
        def turn(n, carry):
            for j in range(TOGETHER):
                tile_copy(part, n * TOGETHER + j).wait_recv()
            work(part, n * TOGETHER)
            return carry

        if start == 0:
            for j in range(1, TOGETHER):
                tile_copy(part, j).wait_recv()
            work(part, 0)
        lax.fori_loop(max(start, 1), stop, turn, 0)

    sent = []

    def go(copy):
        copy.start()
        sent.append(copy)

    order = []
    for t in range(1, half):
        order += [half - t, half + t]
    order += [0]

    def partial(part, ahead, c, b):
        g = (shift(y, ahead, ny) * 2 + c) * 2 + b
        return sums[plan_s[places, part * 2 * n_split + g]]

    def first(part, way, c, h):
        at = (part, way, c, h)
        to = ((above, above_other), (below, below_other))[way][c]
        return remote(first_send.at[at], first_recv.at[at], first_ss.at[at], first_rs.at[at], to)

    def later(part, way, t, b, h):
        at = (part, way, t, b, h)
        return remote(later_send.at[at], later_recv.at[at], later_ss.at[at], later_rs.at[at], (above, below)[way])

    def x_copy(part, ahead):
        at = (part, ahead)
        return remote(xsend.at[at], xrecv.at[at], x_ss.at[at], x_rs.at[at], other)

    def begin(part):
        for c in range(2 if part == 0 else 0):
            shares = [partial(part, half, (core, 1 - core)[c], way) for way in range(2)]
            for h in range(PARTS):
                for way in range(2):
                    first_send[part, way, c, h] = shares[way][h * PIECE:(h + 1) * PIECE]
                    go(first(part, way, c, h))
        for ahead in order if part == 0 else [half] + order:
            for b in range(2):
                xsend[part, ahead, b] = partial(part, ahead, 1 - core, b)
            go(x_copy(part, ahead))

    def came(part, way, t, b, h):
        if t == 0 and way != b:
            return 0.0
        if t == 0 and part == 0:
            got = 0.0
            for c in range(2):
                first(part, way, c, h).wait_recv()
                got = got + first_recv[part, way, c, h]
            return got
        later(part, way, t, b, h).wait_recv()
        return later_recv[part, way, t, b, h]

    def lead(part):
        x_copy(part, half).wait_recv()
        for way in range(2):
            term = partial(part, half, core, way) + xrecv[part, half, way]
            for h in range(PARTS):
                later_send[part, way, 0, way, h] = term[h * PIECE:(h + 1) * PIECE]
                go(later(part, way, 0, way, h))

    def forward(part, t):
        x_copy(part, half - t).wait_recv()
        x_copy(part, half + t).wait_recv()
        for step in range(2):
            for way, b in ((0, 1 - step), (1, step)):
                ahead = half - t if way == 0 else half + t
                term = partial(part, ahead, core, b) + xrecv[part, ahead, b]
                for h in range(PARTS):
                    later_send[part, way, t, b, h] = term[h * PIECE:(h + 1) * PIECE] + came(part, way, t - 1, b, h)
                    go(later(part, way, t, b, h))

    def total(part, b, h):
        if b == 0 and h == 0:
            x_copy(part, 0).wait_recv()
        term = partial(part, 0, core, b) + xrecv[part, 0, b]
        return term[h * PIECE:(h + 1) * PIECE] + came(part, 0, half - 1, b, h) + came(part, 1, half - 1, b, h)

    def back(b, h):
        at = (b, h)
        return remote(back_send.at[at], back_recv.at[at], back_ss.at[at], back_rs.at[at], (at_row(0, opposite), split))

    groups = places // TOGETHER
    lax.fori_loop(1, places, send_tiles(1), 0)
    turns(0, 0, groups)
    begin(0)
    for t in range(1, half - 1):
        forward(0, t)
    turns(1, 0, groups)
    begin(1)
    if half > 1:
        forward(0, half - 1)
    lead(1)
    for b in range(2):
        for h in range(PARTS):
            back_send[b, h] = total(0, b, h)
            go(back(b, h))
    for t in range(1, half):
        forward(1, t)

    def finish(q, carry):
        label_copy(q).wait_send()
        for part in range(2):
            tile_copy(part, q).wait_send()
        return carry

    lax.fori_loop(1, places, finish, 0)
    to_row = lax.broadcasted_iota(jnp.int32, (B, B), 0)
    from_row = lax.broadcasted_iota(jnp.int32, (B, B), 1)
    swap = (from_row == to_row % 2 * ROWS + to_row // 2).astype(jnp.bfloat16)
    for b in range(2):
        halves = []
        for h in range(PARTS):
            whole = total(1, b, h)
            back(b, h).wait_recv()
            halves.append((whole + back_recv[b, h]).astype(jnp.bfloat16))
        out_ref[pl.ds(b * B, B), :] = jnp.dot(
            swap, jnp.concatenate(halves, axis=0), preferred_element_type=jnp.float32
        ).astype(jnp.bfloat16)
    for copy in sent:
        copy.wait_send()


def on_device(n_row, n_split, tiles, tile_dest, tile_row, tile_col, density):
    count, orbitals = tiles.shape[0], density.shape[1]
    places, ny = n_row // 2, n_split // 2
    half = ny // 2
    groups = tiles.reshape(count // 8, 8, ROWS, LANES).transpose(0, 2, 1, 3)
    hbm = pl.BlockSpec(memory_space=pltpu.HBM)
    f32, i32, bf16 = jnp.float32, jnp.int32, jnp.bfloat16
    vmem, smem, dma = pltpu.VMEM, pltpu.SMEM, pltpu.SemaphoreType.DMA
    return pl.pallas_call(
        functools.partial(kernel, n_row, n_split),
        out_shape=jax.ShapeDtypeStruct((2 * B, orbitals), bf16),
        in_specs=[hbm] * 5,
        out_specs=pl.BlockSpec(memory_space=vmem),
        scratch_shapes=[
            *[vmem((1, count), i32)] * 3,
            vmem(groups.shape, bf16),
            vmem((density.shape[0] // B, B, orbitals), bf16),
            vmem((count, ROWS, LANES), f32),
            vmem((places, LANES), i32),
            smem((places, LANES), i32),
            *[vmem((2, places, CAP * ROWS, LANES), bf16)] * 2,
            *[vmem((places, 1, LANES), i32)] * 2,
            vmem((places + 8, LANES), i32),
            smem((places + 8, LANES), i32),
            vmem((2 * places * CAP + 1, B, orbitals), f32),
            *[vmem((2, ny, 2, B, orbitals), f32)] * 2,
            *[vmem((2, 2, 2, PARTS, PIECE, orbitals), f32)] * 2,
            *[vmem((2, 2, half, 2, PARTS, PIECE, orbitals), f32)] * 2,
            *[vmem((2, PARTS, PIECE, orbitals), f32)] * 2,
            dma((7,)), *[dma((places,))] * 2, *[dma((2, places))] * 2, *[dma((2, ny))] * 2,
            *[dma((2, 2, 2, PARTS))] * 2, *[dma((2, 2, half, 2, PARTS))] * 2, *[dma((2, PARTS))] * 2,
        ],
        compiler_params=pltpu.CompilerParams(
            collective_id=0, has_side_effects=True, vmem_limit_bytes=63 * 2**20
        ),
        cost_estimate=pl.CostEstimate(
            flops=2 * n_row * CAP * B * B * orbitals, bytes_accessed=tiles.size * 2, transcendentals=0
        ),
    )(
        tile_dest.reshape(1, count), tile_row.reshape(1, count), tile_col.reshape(1, count), groups,
        density.reshape(-1, B, orbitals),
    )


def solution(mesh):
    n_row, n_split = mesh.shape["row"], mesh.shape["split"]
    placed = (
        P(("row", "split"), None),
        P(("row", "split"), None),
        P(("row", "split")),
        P(("row", "split")),
        P("split", None),
    )
    return jax.shard_map(
        functools.partial(on_device, n_row, n_split),
        mesh=mesh, in_specs=placed, out_specs=P(("row", "split"), None), check_vma=False,
    )
```

```python
import functools

import jax
import jax.numpy as jnp
from jax import lax
from jax.experimental import pallas as pl
from jax.experimental.pallas import tpu as pltpu
from jax.sharding import PartitionSpec as P

MESH = pl.DeviceIdType.MESH
B = 64
LANES = 128
ROWS = B * B // LANES
CAP = 3
NX = 4
PARTS = 1
PIECE = B // PARTS
TOGETHER = 4


def shift(at, by, size):
    return lax.rem(at + by, size)


def kernel(
    n_row, n_split, dest_hbm, row_hbm, col_hbm, tiles_hbm, dens_hbm, out_ref,
    dest_v, row_v, col_v, tiles_v, dens_ref, tall,
    pack, pack_s, send, recv, lab_send, lab_recv, plan, plan_s, sums,
    xsend, xrecv, first_send, first_recv, later_send, later_recv, back_send, back_recv,
    local_sem, lab_ss, lab_rs, tile_ss, tile_rs, x_ss, x_rs,
    first_ss, first_rs, later_ss, later_rs, back_ss, back_rs,
):
    nz, ny = n_row // NX, n_split // 2
    half, opposite = ny // 2, nz // 2
    places = n_row // 2
    row, split = lax.axis_index("row"), lax.axis_index("split")
    x, z = lax.div(row, nz), lax.rem(row, nz)
    y, core = lax.div(split, 2), lax.rem(split, 2)
    up_y, down_y = shift(y, 1, ny) * 2, shift(y, ny - 1, ny) * 2
    other = (row, y * 2 + 1 - core)
    above, above_other = (row, up_y + core), (row, up_y + 1 - core)
    below, below_other = (row, down_y + core), (row, down_y + 1 - core)

    def at_row(dx, dz):
        return shift(x, dx, NX) * nz + shift(z, dz, nz)

    def place(q, x_of, z_of):
        u = lax.rem(places - q, places)
        k = lax.div(u, NX)
        odd = lax.rem(k, 2)
        px = lax.rem(x_of + lax.rem(u, NX), NX)
        dz = odd * lax.div(k + 1, 2) + (1 - odd) * (nz - lax.div(k, 2))
        flip = lax.div(k, opposite - 1) * lax.rem(px, 2) if opposite > 1 else 0
        dz = dz + flip * (nz - 2 * dz)
        return px, lax.rem(z_of + dz, nz)

    def device(q):
        px, pz = place(q, x, z)
        return px * nz + pz, split

    fetches = []
    for i, (src, dst) in enumerate(
        [(dest_hbm, dest_v), (row_hbm, row_v), (col_hbm, col_v), (tiles_hbm, tiles_v), (dens_hbm, dens_ref)]
    ):
        fetches.append(pltpu.make_async_copy(src, dst, local_sem.at[2 + i]))
        fetches[i].start()

    barrier = pltpu.get_barrier_semaphore()
    reach = opposite // 2
    near = {(dx, dz % nz) for dx in range(NX) for dz in range(-reach, reach + 1)} | {(0, opposite)}
    near = sorted(near - {(0, 0)})
    for dx, dz in near:
        pl.semaphore_signal(barrier, inc=1, device_id=(at_row(dx, dz), split), device_id_type=MESH)
    for peer in (other, above, above_other, below, below_other):
        pl.semaphore_signal(barrier, inc=1, device_id=peer, device_id_type=MESH)

    for i in range(3):
        fetches[i].wait()
    dest = dest_v[...]
    label = 1 + row_v[...] * 16 + col_v[...]
    width = dest.shape[1]
    t_sub = lax.broadcasted_iota(jnp.int32, (width, width), 0)
    t_lane = lax.broadcasted_iota(jnp.int32, (width, width), 1)
    dest_col = jnp.sum(jnp.where(t_sub == t_lane, dest, 0), axis=1, keepdims=True)
    rank = jnp.sum(jnp.where((dest_col == dest) & (t_sub < t_lane), 1, 0), axis=0, keepdims=True)
    q_sub = lax.broadcasted_iota(jnp.int32, (places, LANES), 0)
    lane = lax.broadcasted_iota(jnp.int32, (places, LANES), 1)
    t_of = lax.broadcasted_iota(jnp.int32, (places, width), 1)
    q_of = lax.broadcasted_iota(jnp.int32, (places, 1), 0)
    px, pz = place(q_of, x, z)
    packed = jnp.zeros((places, LANES), jnp.int32)
    for i in range(2 * CAP):
        to = px * nz + (lax.rem(pz + opposite, nz) if i < CAP else pz)
        hit = (to == dest) & (rank == i % CAP)
        which = jnp.sum(jnp.where(hit, t_of, 0), axis=1, keepdims=True)
        tag = jnp.sum(jnp.where(hit, label, 0), axis=1, keepdims=True)
        packed = jnp.where(lane == i, which, jnp.where(lane == 2 * CAP + i, tag, packed))
    pack[...] = packed
    fetch = pltpu.make_async_copy(pack, pack_s, local_sem.at[0])
    fetch.start()

    fetches[3].wait()

    def lay(g, carry):
        group = tiles_v[g].astype(jnp.float32)
        for p in range(ROWS):
            tall[pl.ds(g * 8, 8), p, :] = group[p]
        return carry

    lax.fori_loop(0, tiles_v.shape[0], lay, 0)

    def set_label(q, carry):
        lab_send[q] = pack[pl.ds(q, 1), :]
        return carry

    lax.fori_loop(0, places, set_label, 0)
    lab_recv[0] = lab_send[0]
    fetch.wait()

    pl.semaphore_wait(barrier, len(near) + 5)

    def remote(src, dst, ss, rs, to):
        return pltpu.make_async_remote_copy(
            src_ref=src, dst_ref=dst, send_sem=ss, recv_sem=rs, device_id=to, device_id_type=MESH
        )

    def label_copy(q):
        return remote(lab_send.at[q], lab_recv.at[q], lab_ss.at[q], lab_rs.at[q], device(q))

    def tile_copy(part, q):
        return remote(send.at[part, q], recv.at[part, q], tile_ss.at[part, q], tile_rs.at[part, q], device(q))

    def send_label(q, carry):
        label_copy(q).start()
        return carry

    def blocks_to(ref, part, q):
        for i in range(CAP):
            ref[part, q, pl.ds(i * ROWS, ROWS), :] = tall[pack_s[q, part * CAP + i]].astype(jnp.bfloat16)

    def send_tiles(part):
        def step(q, carry):
            blocks_to(send, part, q)
            tile_copy(part, q).start()
            return carry
        return step

    lax.fori_loop(1, places, send_label, 0)
    lax.fori_loop(1, places, send_tiles(0), 0)
    for part in range(2):
        blocks_to(recv, part, 0)

    def wait_label(q, carry):
        label_copy(q).wait_recv()
        return carry

    lax.fori_loop(1, places, wait_label, 0)
    for q in range(places):
        pack[q:q + 1, :] = lab_recv[q]
    labels = pack[...]
    nothing = 2 * places * CAP
    planned = jnp.zeros((places, LANES), jnp.int32)
    last = jnp.full((places, LANES), -1, jnp.int32)
    for part in range(2):
        rows_of, cols_of, across = [], [], []
        for i in range(CAP):
            tag = jnp.sum(jnp.where(lane == (2 + part) * CAP + i, labels, 0), axis=1, keepdims=True) - 1
            rows_of.append(tag >> 4)
            cols_of.append(tag & 15)
            across.append(jnp.sum(jnp.where(lane == q_sub, rows_of[i], 0), axis=0, keepdims=True))
        base = part * places * CAP
        for i in range(CAP):
            best = jnp.full((places, LANES), -1, jnp.int32)
            for h in range(CAP):
                earlier = (lane <= q_sub) if h < i else (lane < q_sub)
                best = jnp.maximum(best, jnp.where(earlier & (rows_of[i] == across[h]), base + lane * CAP + h, -1))
            before = jnp.max(best, axis=1, keepdims=True)
            before = jnp.where(before < 0, nothing, before)
            at = part * CAP + i
            planned = jnp.where(lane == at, before, jnp.where(lane == 2 * CAP + at, cols_of[i], planned))
            here = (rows_of[i] >= 0) & (rows_of[i] + part * 2 * n_split == lane)
            last = jnp.maximum(last, jnp.where(here, base + q_sub * CAP + i, -1))
    last = jnp.max(last, axis=0, keepdims=True)
    plan[0:places, :] = planned
    plan[places:places + 8, :] = jnp.broadcast_to(jnp.where(last < 0, nothing, last), (8, LANES))
    fetch_plan = pltpu.make_async_copy(plan, plan_s, local_sem.at[1])
    fetch_plan.start()
    sums[nothing] = jnp.zeros((B, sums.shape[2]), jnp.float32)
    fetch_plan.wait()
    fetches[4].wait()

    def work(part, q0):
        for j in range(TOGETHER):
            for i in range(CAP):
                block = recv[part, q0 + j, pl.ds(i * ROWS, ROWS), :]
                lhs = jnp.concatenate([block[:, :B], block[:, B:]], axis=0)
                col = plan_s[q0 + j, (2 + part) * CAP + i]
                sums[(part * places + q0 + j) * CAP + i] = jnp.dot(
                    lhs, dens_ref[col], preferred_element_type=jnp.float32
                )
        for j in range(TOGETHER):
            for i in range(CAP):
                at = (part * places + q0 + j) * CAP + i
                sums[at] = sums[at] + sums[plan_s[q0 + j, part * CAP + i]]

    def turns(part, start, stop):
        def turn(n, carry):
            for j in range(TOGETHER):
                tile_copy(part, n * TOGETHER + j).wait_recv()
            work(part, n * TOGETHER)
            return carry

        if start == 0:
            for j in range(1, TOGETHER):
                tile_copy(part, j).wait_recv()
            work(part, 0)
        lax.fori_loop(max(start, 1), stop, turn, 0)

    sent = []

    def go(copy):
        copy.start()
        sent.append(copy)

    order = []
    for t in range(1, half):
        order += [half - t, half + t]
    order += [0]

    def partial(part, ahead, c, b):
        g = (shift(y, ahead, ny) * 2 + c) * 2 + b
        return sums[plan_s[places, part * 2 * n_split + g]]

    def first(part, way, c, h):
        at = (part, way, c, h)
        to = ((above, above_other), (below, below_other))[way][c]
        return remote(first_send.at[at], first_recv.at[at], first_ss.at[at], first_rs.at[at], to)

    def later(part, way, t, b, h):
        at = (part, way, t, b, h)
        return remote(later_send.at[at], later_recv.at[at], later_ss.at[at], later_rs.at[at], (above, below)[way])

    def x_copy(part, ahead):
        at = (part, ahead)
        return remote(xsend.at[at], xrecv.at[at], x_ss.at[at], x_rs.at[at], other)

    def begin(part):
        for c in range(2 if part == 0 else 0):
            shares = [partial(part, half, (core, 1 - core)[c], way) for way in range(2)]
            for h in range(PARTS):
                for way in range(2):
                    first_send[part, way, c, h] = shares[way][h * PIECE:(h + 1) * PIECE]
                    go(first(part, way, c, h))
        for ahead in order if part == 0 else [half] + order:
            for b in range(2):
                xsend[part, ahead, b] = partial(part, ahead, 1 - core, b)
            go(x_copy(part, ahead))

    def came(part, way, t, b, h):
        if t == 0 and way != b:
            return 0.0
        if t == 0 and part == 0:
            got = 0.0
            for c in range(2):
                first(part, way, c, h).wait_recv()
                got = got + first_recv[part, way, c, h]
            return got
        later(part, way, t, b, h).wait_recv()
        return later_recv[part, way, t, b, h]

    def lead(part):
        x_copy(part, half).wait_recv()
        for way in range(2):
            term = partial(part, half, core, way) + xrecv[part, half, way]
            for h in range(PARTS):
                later_send[part, way, 0, way, h] = term[h * PIECE:(h + 1) * PIECE]
                go(later(part, way, 0, way, h))

    def forward(part, t):
        x_copy(part, half - t).wait_recv()
        x_copy(part, half + t).wait_recv()
        for step in range(2):
            for way, b in ((0, 1 - step), (1, step)):
                ahead = half - t if way == 0 else half + t
                term = partial(part, ahead, core, b) + xrecv[part, ahead, b]
                for h in range(PARTS):
                    later_send[part, way, t, b, h] = term[h * PIECE:(h + 1) * PIECE] + came(part, way, t - 1, b, h)
                    go(later(part, way, t, b, h))

    def total(part, b, h):
        if b == 0 and h == 0:
            x_copy(part, 0).wait_recv()
        term = partial(part, 0, core, b) + xrecv[part, 0, b]
        return term[h * PIECE:(h + 1) * PIECE] + came(part, 0, half - 1, b, h) + came(part, 1, half - 1, b, h)

    def back(b, h):
        at = (b, h)
        return remote(back_send.at[at], back_recv.at[at], back_ss.at[at], back_rs.at[at], (at_row(0, opposite), split))

    groups = places // TOGETHER
    lax.fori_loop(1, places, send_tiles(1), 0)
    turns(0, 0, groups)
    begin(0)
    for t in range(1, half - 1):
        forward(0, t)
    turns(1, 0, groups)
    begin(1)
    lead(1)
    if half > 1:
        forward(0, half - 1)
    for b in range(2):
        for h in range(PARTS):
            back_send[b, h] = total(0, b, h)
            go(back(b, h))
    for t in range(1, half):
        forward(1, t)

    def finish(q, carry):
        label_copy(q).wait_send()
        for part in range(2):
            tile_copy(part, q).wait_send()
        return carry

    lax.fori_loop(1, places, finish, 0)
    to_row = lax.broadcasted_iota(jnp.int32, (B, B), 0)
    from_row = lax.broadcasted_iota(jnp.int32, (B, B), 1)
    swap = (from_row == to_row % 2 * ROWS + to_row // 2).astype(jnp.bfloat16)
    for b in range(2):
        halves = []
        for h in range(PARTS):
            whole = total(1, b, h)
            back(b, h).wait_recv()
            halves.append((whole + back_recv[b, h]).astype(jnp.bfloat16))
        out_ref[pl.ds(b * B, B), :] = jnp.dot(
            swap, jnp.concatenate(halves, axis=0), preferred_element_type=jnp.float32
        ).astype(jnp.bfloat16)
    for copy in sent:
        copy.wait_send()


def on_device(n_row, n_split, tiles, tile_dest, tile_row, tile_col, density):
    count, orbitals = tiles.shape[0], density.shape[1]
    places, ny = n_row // 2, n_split // 2
    half = ny // 2
    groups = tiles.reshape(count // 8, 8, ROWS, LANES).transpose(0, 2, 1, 3)
    hbm = pl.BlockSpec(memory_space=pltpu.HBM)
    f32, i32, bf16 = jnp.float32, jnp.int32, jnp.bfloat16
    vmem, smem, dma = pltpu.VMEM, pltpu.SMEM, pltpu.SemaphoreType.DMA
    return pl.pallas_call(
        functools.partial(kernel, n_row, n_split),
        out_shape=jax.ShapeDtypeStruct((2 * B, orbitals), bf16),
        in_specs=[hbm] * 5,
        out_specs=pl.BlockSpec(memory_space=vmem),
        scratch_shapes=[
            *[vmem((1, count), i32)] * 3,
            vmem(groups.shape, bf16),
            vmem((density.shape[0] // B, B, orbitals), bf16),
            vmem((count, ROWS, LANES), f32),
            vmem((places, LANES), i32),
            smem((places, LANES), i32),
            *[vmem((2, places, CAP * ROWS, LANES), bf16)] * 2,
            *[vmem((places, 1, LANES), i32)] * 2,
            vmem((places + 8, LANES), i32),
            smem((places + 8, LANES), i32),
            vmem((2 * places * CAP + 1, B, orbitals), f32),
            *[vmem((2, ny, 2, B, orbitals), f32)] * 2,
            *[vmem((2, 2, 2, PARTS, PIECE, orbitals), f32)] * 2,
            *[vmem((2, 2, half, 2, PARTS, PIECE, orbitals), f32)] * 2,
            *[vmem((2, PARTS, PIECE, orbitals), f32)] * 2,
            dma((7,)), *[dma((places,))] * 2, *[dma((2, places))] * 2, *[dma((2, ny))] * 2,
            *[dma((2, 2, 2, PARTS))] * 2, *[dma((2, 2, half, 2, PARTS))] * 2, *[dma((2, PARTS))] * 2,
        ],
        compiler_params=pltpu.CompilerParams(
            collective_id=0, has_side_effects=True, vmem_limit_bytes=63 * 2**20
        ),
        cost_estimate=pl.CostEstimate(
            flops=2 * n_row * CAP * B * B * orbitals, bytes_accessed=tiles.size * 2, transcendentals=0
        ),
    )(
        tile_dest.reshape(1, count), tile_row.reshape(1, count), tile_col.reshape(1, count), groups,
        density.reshape(-1, B, orbitals),
    )


def solution(mesh):
    n_row, n_split = mesh.shape["row"], mesh.shape["split"]
    placed = (
        P(("row", "split"), None),
        P(("row", "split"), None),
        P(("row", "split")),
        P(("row", "split")),
        P("split", None),
    )
    return jax.shard_map(
        functools.partial(on_device, n_row, n_split),
        mesh=mesh, in_specs=placed, out_specs=P(("row", "split"), None), check_vma=False,
    )
```
